256 devices in a mesh: hi: 8 (over x, core), lo: 32 (over y, z).
Axes of the slice: x: 4, y: 4, z: 8, core: 2. Of those that a mesh axis runs over, the one named last changes fastest.
Arguments:
- right_side: bfloat16 [32, 491520], P(None, ('hi', 'lo')), may hold values from -4.5 to 6.3125
- point_order: int32 [256, 1920], P(('hi', 'lo')), may hold values from 0 to 1919, each once within a row
- leaf_blocks: bfloat16 [491520, 1920], P(('hi', 'lo')), may hold values from -1 to 6
- bases: bfloat16 [8, 491520, 128], P(None, ('hi', 'lo')), may hold values from -1 to 1
Outputs:
- solution: float32 [32, 491520], P(None, ('hi', 'lo'))
The draws below stay inside these ranges and needn't reach their ends.
All inputs are finite; a program needn't handle non-finite values.
Results may differ from the reference program's by a relative error of at most 0.0003.
Values sent between devices are 32-bit elements; how exact they have to be, the bound alone decides.
A program may use at most 64 MiB of HBM per device.

```python
import math
import jax
import jax.numpy as jnp
from jax import lax

LEAF = 1920
RANK = 128
RHS = 32
ITERS = 3
LEVELS = 8
LEAVES = 256
NPTS = 491520


def point_factor(key, low_end, high_end):
    factor_key = jax.random.fold_in(key, 5)
    return jax.random.uniform(factor_key, (NPTS,), minval=low_end, maxval=high_end)


def draw_right_side(key, part):
    key = jax.random.fold_in(key, 11)
    leaf_number = (jnp.arange(NPTS, dtype=jnp.int32) // LEAF).astype(jnp.float32)
    ramp = 0.6 + 1.2 * leaf_number / (LEAVES - 1)
    noise = 0.5 + jnp.clip(jax.random.normal(key, (RHS, NPTS)), -3.0, 3.0)
    return (noise * ramp[None, :]).astype(jnp.bfloat16)


def draw_leaf_blocks(key, part):
    common = point_factor(key, 0.5, 1.5)
    key = jax.random.fold_in(key, 23)
    sigma = 0.8 / math.sqrt(2.0 * LEAF)
    smooth_scale = 0.6 / LEAF

    def make_leaf(leaf_index):
        leaf_key = jax.random.fold_in(key, leaf_index)
        entries = jnp.clip(jax.random.normal(leaf_key, (LEAF, LEAF)), -4.0, 4.0)
        mirrored = 0.5 * sigma * (entries + entries.T)
        diagonal = 2.9 + 3.0 * jax.random.uniform(jax.random.fold_in(leaf_key, 1), (LEAF,))
        on_diagonal = jnp.arange(LEAF)[:, None] == jnp.arange(LEAF)[None, :]
        factor = lax.dynamic_slice_in_dim(common, (leaf_index * LEAF).astype(jnp.int32), LEAF, 0)
        smooth_part = smooth_scale * factor[:, None] * factor[None, :]
        return (jnp.where(on_diagonal, diagonal[:, None], mirrored) + smooth_part).astype(jnp.bfloat16)
    blocks = lax.map(make_leaf, jnp.arange(LEAVES, dtype=jnp.int32))
    return blocks.reshape(NPTS, LEAF)


def draw_bases(key, part):
    common = point_factor(key, 0.5, 1.5)
    key = jax.random.fold_in(key, 37)
    depth = jnp.arange(LEVELS, dtype=jnp.float32)[:, None, None]
    leading = common[None, :, None] * (math.sqrt(0.6 / LEAF) * jnp.exp2(-0.25 * depth))
    column_scale = jnp.exp(jax.random.uniform(jax.random.fold_in(key, 2), (1, 1, RANK), minval=math.log(0.3), maxval=0.0))
    spread = math.sqrt(1.2) / (math.sqrt(LEAF) + math.sqrt(RANK)) * jnp.exp2(-0.5 * depth) * column_scale
    rough = jnp.clip(jax.random.normal(jax.random.fold_in(key, 3), (LEVELS, NPTS, RANK)), -4.0, 4.0)
    return jnp.concatenate([leading, (rough * spread)[:, :, 1:]], axis=2).astype(jnp.bfloat16)


def setup_inputs(seed: int = 0) -> dict:
    arg_keys = jax.random.split(jax.random.key(seed), 5)
    return {
        "right_side": draw_right_side(jax.random.fold_in(arg_keys[4], 71), 0),
        "point_order": jax.vmap(lambda own: jax.random.permutation(own, LEAF))(jax.random.split(arg_keys[1], LEAVES)).reshape((LEAVES, LEAF)).astype(jnp.int32),
        "leaf_blocks": draw_leaf_blocks(jax.random.fold_in(arg_keys[4], 71), 0),
        "bases": draw_bases(jax.random.fold_in(arg_keys[4], 71), 0),
    }


HIGHEST = lax.Precision.HIGHEST


def split_rows(vector, axis_pos):
    high_part = lax.optimization_barrier(vector.astype(jnp.bfloat16))
    low_part = (vector - high_part.astype(jnp.float32)).astype(jnp.bfloat16)
    return jnp.concatenate([high_part, low_part], axis=axis_pos)


def apply_operator(vector, leaf_blocks, bases):
    rhs_count = vector.shape[0]
    halves = split_rows(vector, 0)
    leaf_ids = jnp.arange(LEAVES, dtype=jnp.int32)

    def near_leaf(leaf_index):
        first_column = (leaf_index * LEAF).astype(jnp.int32)
        columns = lax.dynamic_slice_in_dim(halves, first_column, LEAF, 1)
        dense_block = lax.dynamic_slice_in_dim(leaf_blocks, first_column, LEAF, 0)
        basis_rows = lax.dynamic_slice_in_dim(bases, first_column, LEAF, 1)
        near_term = jnp.dot(columns, dense_block, preferred_element_type=jnp.float32)
        projected = jnp.einsum("rp,lpc->lrc", columns.astype(jnp.float32), basis_rows.astype(jnp.float32), precision=HIGHEST)
        return near_term, projected[:, :rhs_count] + projected[:, rhs_count:]

    near_all, projected = lax.map(near_leaf, leaf_ids)
    sibling_list = []
    for depth in range(LEVELS):
        width_leaves = 2 ** depth
        pair_count = LEAVES // (2 * width_leaves)
        node_sums = projected[:, depth].reshape(pair_count, 2, width_leaves, rhs_count, RANK).sum(axis=2)
        swapped = node_sums[:, ::-1]
        spread_out = jnp.broadcast_to(swapped[:, :, None], (pair_count, 2, width_leaves, rhs_count, RANK))
        sibling_list.append(spread_out.reshape(LEAVES, rhs_count, RANK))
    siblings = jnp.stack(sibling_list, axis=1)
    sibling_halves = split_rows(siblings, 2)

    def far_leaf(leaf_index):
        first_column = (leaf_index * LEAF).astype(jnp.int32)
        basis_rows = lax.dynamic_slice_in_dim(bases, first_column, LEAF, 1)
        sums_here = sibling_halves[leaf_index]
        return jnp.einsum("lrc,lpc->rp", sums_here.astype(jnp.float32), basis_rows.astype(jnp.float32), precision=HIGHEST)

    far_all = lax.map(far_leaf, leaf_ids)
    combined = near_all + far_all
    result = combined[:, :rhs_count] + combined[:, rhs_count:]
    return jnp.transpose(result, (1, 0, 2)).reshape(rhs_count, LEAVES * LEAF)


def reference(right_side, point_order, leaf_blocks, bases):
    initial = (jnp.arange(LEAVES, dtype=jnp.int32)[:, None] * LEAF + point_order).reshape(-1).astype(jnp.int32)
    tree_rhs = right_side[:, initial].astype(jnp.float32)
    solution = jnp.zeros_like(tree_rhs)
    residual = tree_rhs
    direction = tree_rhs
    norm_now = jnp.sum(residual * residual, axis=1)
    for iteration in range(ITERS):
        images = apply_operator(direction, leaf_blocks, bases)
        step_size = norm_now / jnp.sum(direction * images, axis=1)
        solution = solution + step_size[:, None] * direction
        residual = residual - step_size[:, None] * images
        norm_next = jnp.sum(residual * residual, axis=1)
        direction = residual + (norm_next / norm_now)[:, None] * direction
        norm_now = norm_next
    return jnp.zeros_like(solution).at[:, initial].set(solution)
```

```python
import functools

import jax
import jax.numpy as jnp
from jax import lax
from jax.experimental import pallas as pl
from jax.experimental.pallas import tpu as pltpu
from jax.sharding import PartitionSpec as P

ITERS = 3
Z_COUNT = 8
MESH = pl.DeviceIdType.MESH
F32 = jnp.float32
BF16 = jnp.bfloat16
NN = (((1,), (0,)), ((), ()))
NT = (((1,), (1,)), ((), ()))


def bits(count):
    return count.bit_length() - 1


def spans(total, width):
    return [(low, min(width, total - low)) for low in range(0, total, width)]


def split(value):
    high = value.astype(BF16)
    low = (value - high.astype(F32)).astype(BF16)
    return high, low


def product(left, right, numbers):
    rows = left.shape[0] // 2
    both = lax.dot_general(left, right, numbers, preferred_element_type=F32)
    return both[:rows] + both[rows:]


def row_dot(a, b):
    return jnp.sum(a * b, axis=1, keepdims=True)


def pack_columns(columns):
    groups = columns[0].shape[0] // 8
    lane = lax.broadcasted_iota(jnp.int32, (8, 128), 1)
    tile = jnp.zeros((8, 128), F32)
    for kind, column in enumerate(columns):
        for group in range(groups):
            part = column[8 * group:8 * group + 8]
            tile = jnp.where(lane == kind * groups + group, part, tile)
    return tile


def unpack_column(tile, kind, groups):
    first = kind * groups
    parts = [tile[:, first + group:first + group + 1] for group in range(groups)]
    return jnp.concatenate(parts, axis=0)


def tree_steps(blocks, first_level, per_level):
    rows = blocks[0].shape[0]
    level_of_row = lax.broadcasted_iota(jnp.int32, (rows, 128), 0) // per_level
    products = jnp.zeros((rows, 128), F32)
    node_sums = []
    current = blocks
    level = first_level
    while len(current) > 1:
        node_sums.append(current)
        pairs = [(current[m], current[m + 1]) for m in range(0, len(current), 2)]
        total = sum(a * b for a, b in pairs)
        products = products + jnp.where(level_of_row == level, total, 0.0)
        current = [a + b for a, b in pairs]
        level += 1
    return node_sums, current[0], products


def fold_levels(products, per_level):
    column = jnp.sum(products, axis=1, keepdims=True)
    total = column[:per_level]
    for low in range(per_level, products.shape[0], per_level):
        total = total + column[low:low + per_level]
    return 2.0 * total


def kernel(dims, rhs_ref, order_ref, leaf_hbm, bases_hbm, out_ref, *scratch):
    nz, ny, nh = dims
    (blocks, basis, onehot, halves, sib_f32, sib_halves, residual, direction, image, far_dir,
     near, placed, pending, near_send, z_recv, y_send, y_recv, h_send, h_recv, a_send, a_recv, b_send,
     b_recv, last_recv, load_sem, send_sem, recv_sem) = scratch
    rhs_count, leaf = residual.shape
    levels = bases_hbm.shape[0]
    own = rhs_count // nz
    groups = rhs_count // 8
    zb, yb = bits(nz), bits(ny)
    z_rows = levels * own
    h_low = (zb + yb) * own // 8 * 8
    a_rows = zb * own

    hi = lax.axis_index("hi")
    lo = lax.axis_index("lo")
    z = lax.rem(lo, nz)
    y = lo // nz

    def z_peer(step):
        return lax.rem(z + step, nz)

    def y_peer(step):
        return lax.rem(y + step, ny)

    def h_peer(step):
        return lax.rem(hi + step, nh)

    partners = [(hi, y * nz + z_peer(step)) for step in range(1, nz)]
    partners += [(hi, y_peer(step) * nz + z) for step in range(1, ny)]
    partners += [(h_peer(step), lo) for step in range(1, nh)]

    loads = []
    for level in range(levels):
        loads.append(pltpu.make_async_copy(
            bases_hbm.at[level], basis.at[:, pl.ds(128 * level, 128)], load_sem.at[level]))
    loads.append(pltpu.make_async_copy(leaf_hbm, blocks, load_sem.at[levels]))
    for load in loads:
        load.start()

    barrier = pltpu.get_barrier_semaphore()
    for partner in partners:
        pl.semaphore_signal(barrier, inc=1, device_id=partner, device_id_type=MESH)

    def send(src, dst, t, phase, partner):
        pltpu.make_async_remote_copy(
            src_ref=src, dst_ref=dst, send_sem=send_sem.at[t, phase],
            recv_sem=recv_sem.at[t, phase], device_id=partner, device_id_type=MESH,
        ).start()

    def await_recv(slots, t, phase):
        pltpu.make_async_copy(slots, slots, recv_sem.at[t, phase]).wait()

    def await_send(slots, t, phase):
        pltpu.make_async_copy(slots, slots, send_sem.at[t, phase]).wait()

    order_row = order_ref[...]
    for low, width in spans(leaf, 128):
        place = lax.broadcasted_iota(jnp.int32, (width, leaf), 0) + low
        onehot[pl.ds(low, width), :] = jnp.where(place == order_row, 1.0, 0.0).astype(BF16)
    rhs_now = rhs_ref[...]
    for low, width in spans(leaf, 384):
        columns = pl.ds(low, width)
        tree = lax.dot_general(rhs_now, onehot[:, columns], NN, preferred_element_type=F32)
        residual[:, columns] = tree
        high, small = split(tree)
        halves[:, columns] = jnp.concatenate([high, small], axis=0)
    direction[...] = jnp.zeros_like(direction)
    image[...] = jnp.zeros_like(image)
    far_dir[...] = jnp.zeros_like(far_dir)
    placed[...] = jnp.zeros_like(placed)
    out_ref[...] = jnp.zeros_like(out_ref)

    for load in loads[:levels]:
        load.wait()

    def exchange(t, first, last):
        projected = product(halves[...], basis[...], NN)
        for j in range(nz):
            for level in range(levels):
                near_send[t, j, own * level:own * level + own, :] = (
                    projected[own * j:own * j + own, 128 * level:128 * level + 128])
        if first:
            pl.semaphore_wait(barrier, len(partners))
        for step in range(1, nz):
            peer = z_peer(step)
            send(near_send.at[t, peer], z_recv.at[t, z], t, 0, (hi, y * nz + peer))
        z_recv[t, z] = near_send[t, z]
        if first:
            loads[levels].wait()

        rr = jnp.zeros((rhs_count, 1), F32)
        rn = jnp.zeros((rhs_count, 1), F32)
        cross = jnp.zeros((rhs_count, 1), F32)
        for low, width in spans(leaf, 384):
            columns = pl.ds(low, width)
            near_now = product(halves[...], blocks[:, columns], NN)
            near[:, columns] = near_now
            r_now = residual[:, columns]
            rr = rr + row_dot(r_now, r_now)
            rn = rn + row_dot(r_now, near_now)
            cross = cross + row_dot(r_now, image[:, columns] + far_dir[:, columns])
            cross = cross + row_dot(direction[:, columns], near_now)
        tile = pack_columns([rr, rn, cross])

        lane = lax.broadcasted_iota(jnp.int32, (8, 128), 1)
        sub = lax.broadcasted_iota(jnp.int32, (8, 128), 0)
        mine = (lane == groups + z * own // 8) & (sub // own == lax.rem(z, 8 // own))

        def add_products(tile, products):
            dots = fold_levels(products, own)
            repeated = jnp.concatenate([dots] * (8 // own), axis=0)
            return tile + jnp.where(mine, repeated, 0.0)

        await_recv(z_recv.at[t, pl.ds(0, nz - 1)], t, 0)
        node_sums, total, products = tree_steps([z_recv[t, j] for j in range(nz)], 0, own)
        tile = add_products(tile, products)
        y_send[t, 0:8] = tile
        y_send[t, 8:z_rows] = total[8:]
        for step in range(1, ny):
            peer = y_peer(step)
            send(y_send.at[t], y_recv.at[t, y], t, 1, (hi, peer * nz + z))
        y_recv[t, y] = y_send[t]
        if not last:
            for j in range(nz):
                for level in range(zb):
                    rows = slice(own * level, own * level + own)
                    a_send[t, j, rows] = node_sums[level][(j >> level) ^ 1][rows]
            for step in range(1, nz):
                peer = z_peer(step)
                send(a_send.at[t, peer], a_recv.at[t, z], t, 3, (hi, y * nz + peer))
            a_recv[t, z] = a_send[t, z]

        if not first:
            place_chunk(0)

        await_recv(y_recv.at[t, pl.ds(0, ny - 1)], t, 1)
        _, total, products = tree_steps([y_recv[t, j] for j in range(ny)], zb, own)
        tile = add_products(total[0:8], products)
        h_send[t, 0:8] = tile
        h_send[t, 8:] = total[h_low:]
        for step in range(1, nh):
            send(h_send.at[t], h_recv.at[t, hi], t, 2, (h_peer(step), lo))
        h_recv[t, hi] = h_send[t]
        if not last:
            for level in range(yb):
                rows = slice(own * (zb + level), own * (zb + level) + own)
                first_node = ((y >> level) + 1 - 2 * lax.rem(y >> level, 2)) << level
                found = y_recv[t, first_node, rows]
                for extra in range(1, 1 << level):
                    found = found + y_recv[t, first_node + extra, rows]
                b_send[t, rows] = found

        if not first:
            place_chunk(1)

        await_recv(h_recv.at[t, pl.ds(0, nh - 1)], t, 2)
        first_hi = (zb + yb) * own - h_low + 8
        blocks_h = [h_recv[t, j] for j in range(nh)]
        _, total, products = tree_steps(blocks_h, first_hi // own, own)
        tile = add_products(total[0:8], products)
        b_send[t, 0:8] = tile
        if last:
            for step in range(1, nz):
                peer = z_peer(step)
                send(b_send.at[t, pl.ds(0, 8)], last_recv.at[z], t, 4, (hi, y * nz + peer))
            last_recv[z] = tile
            place_chunk(2)
            await_recv(last_recv.at[pl.ds(0, nz - 1)], t, 4)
            tile = sum(last_recv[j] for j in range(nz))
        else:
            for level in range(bits(nh)):
                rows = slice(own * (zb + yb + level), own * (zb + yb + level) + own)
                from_rows = slice(first_hi + own * level, first_hi + own * level + own)
                first_node = ((hi >> level) + 1 - 2 * lax.rem(hi >> level, 2)) << level
                found = h_recv[t, first_node, from_rows]
                for extra in range(1, 1 << level):
                    found = found + h_recv[t, first_node + extra, from_rows]
                b_send[t, rows] = found
            for step in range(1, nz):
                peer = z_peer(step)
                send(b_send.at[t], b_recv.at[t, z], t, 4, (hi, y * nz + peer))
            b_recv[t, z] = b_send[t]
            if not first:
                place_chunk(2)
            await_recv(a_recv.at[t, pl.ds(0, nz - 1)], t, 3)
            await_recv(b_recv.at[t, pl.ds(0, nz - 1)], t, 4)
            tile = b_recv[t, 0, 0:8]
            for j in range(1, nz):
                tile = tile + b_recv[t, j, 0:8]
            for j in range(nz):
                for level in range(levels):
                    source = a_recv if level < zb else b_recv
                    sib_f32[own * j:own * j + own, 128 * level:128 * level + 128] = (
                        source[t, j, own * level:own * level + own, :])
            high, small = split(sib_f32[...])
            sib_halves[...] = jnp.concatenate([high, small], axis=0)
        return [unpack_column(tile, kind, groups) for kind in range(3)]

    third = leaf // 3

    def place_chunk(number):
        for low, width in spans(third, 640):
            rows = pl.ds(number * third + low, width)
            pending[:, rows] = product(halves[...], onehot[rows, :], NT)

    rr_old = jnp.ones((rhs_count, 1), F32)
    curvature = jnp.zeros((rhs_count, 1), F32)
    for t in range(ITERS):
        first, last = t == 0, t == ITERS - 1
        rr, rn, cross = exchange(t, first, last)
        beta = jnp.zeros_like(rr) if first else rr / rr_old
        curvature = rn + beta * cross + beta * beta * curvature
        alpha = rr / curvature
        rr_old = rr
        here = rhs_now.astype(F32) if first else pending[...]
        place_now = here + beta * placed[...]
        placed[...] = place_now
        out_ref[...] = out_ref[...] + alpha * place_now
        if last:
            break
        for low, width in spans(leaf, 384):
            columns = pl.ds(low, width)
            far = product(sib_halves[...], basis[columns, :], NT)
            far_now = far + beta * far_dir[:, columns]
            far_dir[:, columns] = far_now
            image_now = near[:, columns] + far + beta * image[:, columns]
            image[:, columns] = image_now
            r_now = residual[:, columns]
            direction[:, columns] = r_now + beta * direction[:, columns]
            r_next = r_now - alpha * image_now
            residual[:, columns] = r_next
            high, small = split(r_next)
            halves[:, columns] = jnp.concatenate([high, small], axis=0)

    for t in range(ITERS):
        await_send(z_recv.at[t, pl.ds(0, nz - 1)], t, 0)
        await_send(y_recv.at[t, pl.ds(0, ny - 1)], t, 1)
        await_send(h_recv.at[t, pl.ds(0, nh - 1)], t, 2)
        if t < ITERS - 1:
            await_send(a_recv.at[t, pl.ds(0, nz - 1)], t, 3)
            await_send(b_recv.at[t, pl.ds(0, nz - 1)], t, 4)
        else:
            await_send(last_recv.at[pl.ds(0, nz - 1)], t, 4)


def per_device(dims, right_side, point_order, leaf_blocks, bases):
    nz, ny, nh = dims
    rhs_count, leaf = right_side.shape
    levels = bases.shape[0]
    own = rhs_count // nz
    z_rows = levels * own
    h_rows = 8 + z_rows - (bits(nz) + bits(ny)) * own // 8 * 8
    a_rows = bits(nz) * own
    vector = pltpu.VMEM((rhs_count, leaf), F32)
    scratch = [
        pltpu.VMEM((leaf, leaf), BF16),
        pltpu.VMEM((leaf, 128 * levels), BF16),
        pltpu.VMEM((leaf, leaf), BF16),
        pltpu.VMEM((2 * rhs_count, leaf), BF16),
        pltpu.VMEM((rhs_count, 128 * levels), F32),
        pltpu.VMEM((2 * rhs_count, 128 * levels), BF16),
        vector, vector, vector, vector, vector, vector, vector,
        pltpu.VMEM((ITERS, nz, z_rows, 128), F32),
        pltpu.VMEM((ITERS, nz, z_rows, 128), F32),
        pltpu.VMEM((ITERS, z_rows, 128), F32),
        pltpu.VMEM((ITERS, ny, z_rows, 128), F32),
        pltpu.VMEM((ITERS, h_rows, 128), F32),
        pltpu.VMEM((ITERS, nh, h_rows, 128), F32),
        pltpu.VMEM((ITERS, nz, a_rows, 128), F32),
        pltpu.VMEM((ITERS, nz, a_rows, 128), F32),
        pltpu.VMEM((ITERS, z_rows, 128), F32),
        pltpu.VMEM((ITERS, nz, z_rows, 128), F32),
        pltpu.VMEM((nz, 8, 128), F32),
        pltpu.SemaphoreType.DMA((levels + 1,)),
        pltpu.SemaphoreType.DMA((ITERS, 5)),
        pltpu.SemaphoreType.DMA((ITERS, 5)),
    ]
    return pl.pallas_call(
        functools.partial(kernel, dims),
        out_shape=jax.ShapeDtypeStruct((rhs_count, leaf), F32),
        in_specs=[
            pl.BlockSpec(memory_space=pltpu.VMEM),
            pl.BlockSpec(memory_space=pltpu.VMEM),
            pl.BlockSpec(memory_space=pl.ANY),
            pl.BlockSpec(memory_space=pl.ANY),
        ],
        out_specs=pl.BlockSpec(memory_space=pltpu.VMEM),
        scratch_shapes=scratch,
        compiler_params=pltpu.CompilerParams(
            collective_id=0, has_side_effects=True, vmem_limit_bytes=48 * 1024 * 1024
        ),
        name="tree_cg",
    )(right_side, point_order, leaf_blocks, bases)


def solution(mesh):
    dims = (Z_COUNT, mesh.shape["lo"] // Z_COUNT, mesh.shape["hi"])
    in_specs = (
        P(None, ("hi", "lo")),
        P(("hi", "lo"), None),
        P(("hi", "lo"), None),
        P(None, ("hi", "lo"), None),
    )
    return jax.shard_map(
        functools.partial(per_device, dims), mesh=mesh, in_specs=in_specs,
        out_specs=P(None, ("hi", "lo")), check_vma=False
    )
```

```python
import functools

import jax
import jax.numpy as jnp
from jax import lax
from jax.experimental import pallas as pl
from jax.experimental.pallas import tpu as pltpu
from jax.sharding import PartitionSpec as P

ITERS = 3
Z_COUNT = 8
VMEM_BYTES = 60 * 1024 * 1024
MESH = pl.DeviceIdType.MESH
F32 = jnp.float32
BF16 = jnp.bfloat16
NN = (((1,), (0,)), ((), ()))
NT = (((1,), (1,)), ((), ()))


def bits(count):
    return count.bit_length() - 1


def spans(total, width):
    return [(low, min(width, total - low)) for low in range(0, total, width)]


def split(value):
    high = value.astype(BF16)
    low = (value - high.astype(F32)).astype(BF16)
    return high, low


def product(left, right, numbers):
    rows = left.shape[0] // 2
    both = lax.dot_general(left, right, numbers, preferred_element_type=F32)
    return both[:rows] + both[rows:]


def row_dot(a, b):
    return jnp.sum(a * b, axis=1, keepdims=True)


def pack_columns(columns):
    count = columns[0].shape[0]
    lane = lax.broadcasted_iota(jnp.int32, (count, 128), 1)
    row = lax.broadcasted_iota(jnp.int32, (count, 128), 0)
    spread = jnp.zeros((count, 128), F32)
    for kind, column in enumerate(columns):
        spread = jnp.where(lane == row + kind * count, column, spread)
    return jnp.sum(spread, axis=0, keepdims=True)


def unpack_column(packed, kind, count):
    lane = lax.broadcasted_iota(jnp.int32, (count, 128), 1)
    row = lax.broadcasted_iota(jnp.int32, (count, 128), 0)
    picked = jnp.where(lane == row + kind * count, packed, 0.0)
    return jnp.sum(picked, axis=1, keepdims=True)


def tree_steps(blocks, first_level, per_level):
    rows = blocks[0].shape[0]
    level_of_row = lax.broadcasted_iota(jnp.int32, (rows, 128), 0) // per_level
    products = jnp.zeros((rows, 128), F32)
    node_sums = []
    current = blocks
    level = first_level
    while len(current) > 1:
        node_sums.append(current)
        pairs = [(current[m], current[m + 1]) for m in range(0, len(current), 2)]
        total = sum(a * b for a, b in pairs)
        products = products + jnp.where(level_of_row == level, total, 0.0)
        current = [a + b for a, b in pairs]
        level += 1
    return node_sums, current[0], products


def fold_levels(products, per_level):
    column = jnp.sum(products, axis=1, keepdims=True)
    total = column[:per_level]
    for low in range(per_level, products.shape[0], per_level):
        total = total + column[low:low + per_level]
    return 2.0 * total


def kernel(dims, rhs_hbm, order_hbm, leaf_hbm, bases_hbm, out_ref, *scratch):
    nz, ny, nh = dims
    (rhs_ref, order_ref, blocks, basis, onehot, halves, sib_f32, sib_halves, residual, direction,
     image, far_dir, near, placed, pending, c_send, c_recv, l_send, l_recv, y_send, y_recv, h_send,
     h_recv, a_send, a_recv, b_send, b_recv, s_send, sy_recv, sh_recv, sz_recv, load_sem, send_sem,
     recv_sem) = scratch
    rhs_count, leaf = residual.shape
    levels = bases_hbm.shape[0]
    own = rhs_count // nz
    zb, yb, hb = bits(nz), bits(ny), bits(nh)
    c_rows = c_send.shape[2]
    h_low = yb * own // 8 * 8
    h_first = yb * own - h_low

    hi = lax.axis_index("hi")
    lo = lax.axis_index("lo")
    z = lax.rem(lo, nz)
    y = lo // nz

    z_steps = sorted(range(1, nz), key=lambda step: -min(step, nz - step))
    y_steps = sorted(range(1, ny), key=lambda step: -min(step, ny - step))
    h_steps = sorted(range(1, nh), key=lambda step: -min(step, nh - step))

    def z_device(step):
        return (hi, y * nz + lax.rem(z + step, nz))

    def y_device(step):
        return (hi, lax.rem(y + step, ny) * nz + z)

    def h_device(step):
        return (lax.rem(hi + step, nh), lo)

    partners = [z_device(step) for step in z_steps]
    partners += [y_device(step) for step in y_steps]
    partners += [h_device(step) for step in h_steps]

    loads = []
    for level in range(levels):
        loads.append(pltpu.make_async_copy(
            bases_hbm.at[level], basis.at[:, pl.ds(128 * level, 128)], load_sem.at[level]))
    loads.append(pltpu.make_async_copy(leaf_hbm, blocks, load_sem.at[levels]))
    loads.insert(0, pltpu.make_async_copy(rhs_hbm, rhs_ref, load_sem.at[levels + 1]))
    loads.insert(0, pltpu.make_async_copy(order_hbm, order_ref, load_sem.at[levels + 2]))
    for load in loads:
        load.start()

    barrier = pltpu.get_barrier_semaphore()
    for partner in partners:
        pl.semaphore_signal(barrier, inc=1, device_id=partner, device_id_type=MESH)

    def send(src, dst, t, phase, partner):
        pltpu.make_async_remote_copy(
            src_ref=src, dst_ref=dst, send_sem=send_sem.at[t, phase],
            recv_sem=recv_sem.at[t, phase], device_id=partner, device_id_type=MESH,
        ).start()

    def await_recv(slots, t, phase):
        pltpu.make_async_copy(slots, slots, recv_sem.at[t, phase]).wait()

    def await_send(slots, t, phase):
        pltpu.make_async_copy(slots, slots, send_sem.at[t, phase]).wait()

    for load in loads[:2]:
        load.wait()
    order_row = order_ref[...]
    for low, width in spans(leaf, 128):
        place = lax.broadcasted_iota(jnp.int32, (width, leaf), 0) + low
        onehot[pl.ds(low, width), :] = jnp.where(place == order_row, 1.0, 0.0).astype(BF16)
    rhs_now = rhs_ref[...]
    for low, width in spans(leaf, 384):
        columns = pl.ds(low, width)
        tree = lax.dot_general(rhs_now, onehot[:, columns], NN, preferred_element_type=F32)
        residual[:, columns] = tree
        high, small = split(tree)
        halves[:, columns] = jnp.concatenate([high, small], axis=0)
    direction[...] = jnp.zeros_like(direction)
    image[...] = jnp.zeros_like(image)
    far_dir[...] = jnp.zeros_like(far_dir)
    placed[...] = jnp.zeros_like(placed)
    out_ref[...] = jnp.zeros_like(out_ref)

    for load in loads[2:levels + 2]:
        load.wait()

    def exchange(t, first, last):
        projected = product(halves[...], basis[...], NN)
        for j in range(nz):
            for level in range(levels):
                target, at = (l_send, level) if level < zb else (c_send, level - zb)
                target[t, j, own * at:own * at + own, :] = (
                    projected[own * j:own * j + own, 128 * level:128 * level + 128])
        if first:
            pl.semaphore_wait(barrier, len(partners))
        for step in z_steps:
            peer = lax.rem(z + step, nz)
            send(c_send.at[t, peer], c_recv.at[t, z], t, 0, z_device(step))
        for step in z_steps:
            peer = lax.rem(z + step, nz)
            send(l_send.at[t, peer], l_recv.at[t, z], t, 1, z_device(step))
        c_recv[t, z] = c_send[t, z]
        l_recv[t, z] = l_send[t, z]
        if first:
            loads[levels + 2].wait()

        rr = jnp.zeros((rhs_count, 1), F32)
        rn = jnp.zeros((rhs_count, 1), F32)
        cross = jnp.zeros((rhs_count, 1), F32)
        for low, width in spans(leaf, 384):
            columns = pl.ds(low, width)
            near_now = product(halves[...], blocks[:, columns], NN)
            near[:, columns] = near_now
            r_now = residual[:, columns]
            rr = rr + row_dot(r_now, r_now)
            rn = rn + row_dot(r_now, near_now)
            if not first:
                cross = cross + row_dot(r_now, image[:, columns] + far_dir[:, columns])
                cross = cross + row_dot(direction[:, columns], near_now)
        packed = pack_columns([rr, rn, cross])

        lane = lax.broadcasted_iota(jnp.int32, (own, 128), 1)
        row = lax.broadcasted_iota(jnp.int32, (own, 128), 0)
        mine = lane == row + rhs_count + z * own

        def add_products(packed, products):
            placed_dots = jnp.where(mine, fold_levels(products, own), 0.0)
            return packed + jnp.sum(placed_dots, axis=0, keepdims=True)

        await_recv(c_recv.at[t, pl.ds(0, nz - 1)], t, 0)
        total = c_recv[t, 0]
        for j in range(1, nz):
            total = total + c_recv[t, j]
        y_send[t] = total
        for step in y_steps:
            send(y_send.at[t], y_recv.at[t, y], t, 2, y_device(step))
        y_recv[t, y] = total

        await_recv(l_recv.at[t, pl.ds(0, nz - 1)], t, 1)
        node_sums, _, products = tree_steps([l_recv[t, j] for j in range(nz)], 0, own)
        packed = add_products(packed, products)
        s_send[t, 0] = packed
        for step in y_steps:
            send(s_send.at[t, 0], sy_recv.at[t, y], t, 3, y_device(step))
        sy_recv[t, y] = packed
        if not last:
            for j in range(nz):
                for level in range(zb):
                    rows = slice(own * level, own * level + own)
                    a_send[t, j, rows] = node_sums[level][(j >> level) ^ 1][rows]
            for step in z_steps:
                peer = lax.rem(z + step, nz)
                send(a_send.at[t, peer], a_recv.at[t, z], t, 4, z_device(step))
            a_recv[t, z] = a_send[t, z]
        if not first:
            place_chunk(0)

        await_recv(y_recv.at[t, pl.ds(0, ny - 1)], t, 2)
        _, total, products = tree_steps([y_recv[t, j] for j in range(ny)], 0, own)
        h_send[t] = total[h_low:]
        for step in h_steps:
            send(h_send.at[t], h_recv.at[t, hi], t, 5, h_device(step))
        h_recv[t, hi] = h_send[t]
        await_recv(sy_recv.at[t, pl.ds(0, ny - 1)], t, 3)
        packed = sum(sy_recv[t, j] for j in range(ny))
        packed = add_products(packed, products)
        s_send[t, 1] = packed
        for step in h_steps:
            send(s_send.at[t, 1], sh_recv.at[t, hi], t, 6, h_device(step))
        sh_recv[t, hi] = packed
        if not last:
            for level in range(yb):
                rows = slice(own * level, own * level + own)
                first_node = ((y >> level) + 1 - 2 * lax.rem(y >> level, 2)) << level
                found = y_recv[t, first_node, rows]
                for extra in range(1, 1 << level):
                    found = found + y_recv[t, first_node + extra, rows]
                b_send[t, rows] = found
        if not first:
            place_chunk(1)

        await_recv(h_recv.at[t, pl.ds(0, nh - 1)], t, 5)
        if not last:
            for level in range(hb):
                from_rows = slice(h_first + own * level, h_first + own * level + own)
                first_node = ((hi >> level) + 1 - 2 * lax.rem(hi >> level, 2)) << level
                found = h_recv[t, first_node, from_rows]
                for extra in range(1, 1 << level):
                    found = found + h_recv[t, first_node + extra, from_rows]
                b_send[t, own * (yb + level):own * (yb + level) + own] = found
            for step in z_steps:
                send(b_send.at[t], b_recv.at[t, z], t, 7, z_device(step))
            b_recv[t, z] = b_send[t]
        _, _, products = tree_steps([h_recv[t, j] for j in range(nh)], h_first // own, own)
        await_recv(sh_recv.at[t, pl.ds(0, nh - 1)], t, 6)
        packed = sum(sh_recv[t, j] for j in range(nh))
        packed = add_products(packed, products)
        s_send[t, 2] = packed
        for step in z_steps:
            send(s_send.at[t, 2], sz_recv.at[t, z], t, 8, z_device(step))
        sz_recv[t, z] = packed
        if not first:
            place_chunk(2)

        if not last:
            await_recv(a_recv.at[t, pl.ds(0, nz - 1)], t, 4)
            await_recv(b_recv.at[t, pl.ds(0, nz - 1)], t, 7)
            for j in range(nz):
                for level in range(levels):
                    source, at = (a_recv, level) if level < zb else (b_recv, level - zb)
                    sib_f32[own * j:own * j + own, 128 * level:128 * level + 128] = (
                        source[t, j, own * at:own * at + own, :])
            high, small = split(sib_f32[...])
            sib_halves[...] = jnp.concatenate([high, small], axis=0)
        await_recv(sz_recv.at[t, pl.ds(0, nz - 1)], t, 8)
        packed = sum(sz_recv[t, j] for j in range(nz))
        return [unpack_column(packed, kind, rhs_count) for kind in range(3)]

    third = leaf // 3

    def place_chunk(number):
        for low, width in spans(third, 640):
            rows = pl.ds(number * third + low, width)
            pending[:, rows] = product(halves[...], onehot[rows, :], NT)

    rr_old = jnp.ones((rhs_count, 1), F32)
    curvature = jnp.zeros((rhs_count, 1), F32)
    for t in range(ITERS):
        first, last = t == 0, t == ITERS - 1
        rr, rn, cross = exchange(t, first, last)
        beta = jnp.zeros_like(rr) if first else rr / rr_old
        curvature = rn + beta * cross + beta * beta * curvature
        alpha = rr / curvature
        rr_old = rr
        here = rhs_now.astype(F32) if first else pending[...]
        place_now = here + beta * placed[...]
        placed[...] = place_now
        out_ref[...] = out_ref[...] + alpha * place_now
        if last:
            break
        for low, width in spans(leaf, 384):
            columns = pl.ds(low, width)
            far = product(sib_halves[...], basis[columns, :], NT)
            far_now = far + beta * far_dir[:, columns]
            far_dir[:, columns] = far_now
            image_now = near[:, columns] + far + beta * image[:, columns]
            image[:, columns] = image_now
            r_now = residual[:, columns]
            direction[:, columns] = r_now + beta * direction[:, columns]
            r_next = r_now - alpha * image_now
            residual[:, columns] = r_next
            high, small = split(r_next)
            halves[:, columns] = jnp.concatenate([high, small], axis=0)

    for t in range(ITERS):
        await_send(c_recv.at[t, pl.ds(0, nz - 1)], t, 0)
        await_send(l_recv.at[t, pl.ds(0, nz - 1)], t, 1)
        await_send(y_recv.at[t, pl.ds(0, ny - 1)], t, 2)
        await_send(sy_recv.at[t, pl.ds(0, ny - 1)], t, 3)
        await_send(h_recv.at[t, pl.ds(0, nh - 1)], t, 5)
        await_send(sh_recv.at[t, pl.ds(0, nh - 1)], t, 6)
        await_send(sz_recv.at[t, pl.ds(0, nz - 1)], t, 8)
        if t < ITERS - 1:
            await_send(a_recv.at[t, pl.ds(0, nz - 1)], t, 4)
            await_send(b_recv.at[t, pl.ds(0, nz - 1)], t, 7)


def per_device(dims, right_side, point_order, leaf_blocks, bases):
    nz, ny, nh = dims
    rhs_count, leaf = right_side.shape
    levels = bases.shape[0]
    own = rhs_count // nz
    yb = bits(ny)
    l_rows = bits(nz) * own
    c_rows = levels * own - l_rows
    h_rows = c_rows - yb * own // 8 * 8
    vector = pltpu.VMEM((rhs_count, leaf), F32)

    def buffer(*shape):
        return pltpu.VMEM((ITERS, *shape, 128), F32)

    scratch = [
        pltpu.VMEM((rhs_count, leaf), BF16),
        pltpu.VMEM((1, leaf), jnp.int32),
        pltpu.VMEM((leaf, leaf), BF16),
        pltpu.VMEM((leaf, 128 * levels), BF16),
        pltpu.VMEM((leaf, leaf), BF16),
        pltpu.VMEM((2 * rhs_count, leaf), BF16),
        pltpu.VMEM((rhs_count, 128 * levels), F32),
        pltpu.VMEM((2 * rhs_count, 128 * levels), BF16),
        vector, vector, vector, vector, vector, vector, vector,
        buffer(nz, c_rows), buffer(nz, c_rows),
        buffer(nz, l_rows), buffer(nz, l_rows),
        buffer(c_rows), buffer(ny, c_rows),
        buffer(h_rows), buffer(nh, h_rows),
        buffer(nz, l_rows), buffer(nz, l_rows),
        buffer(c_rows), buffer(nz, c_rows),
        buffer(3, 1), buffer(ny, 1), buffer(nh, 1), buffer(nz, 1),
        pltpu.SemaphoreType.DMA((levels + 3,)),
        pltpu.SemaphoreType.DMA((ITERS, 9)),
        pltpu.SemaphoreType.DMA((ITERS, 9)),
    ]
    return pl.pallas_call(
        functools.partial(kernel, dims),
        out_shape=jax.ShapeDtypeStruct((rhs_count, leaf), F32),
        in_specs=[
            pl.BlockSpec(memory_space=pl.ANY),
            pl.BlockSpec(memory_space=pl.ANY),
            pl.BlockSpec(memory_space=pl.ANY),
            pl.BlockSpec(memory_space=pl.ANY),
        ],
        out_specs=pl.BlockSpec(memory_space=pltpu.VMEM),
        scratch_shapes=scratch,
        compiler_params=pltpu.CompilerParams(
            collective_id=0, has_side_effects=True, vmem_limit_bytes=VMEM_BYTES
        ),
        name="tree_cg",
    )(right_side, point_order, leaf_blocks, bases)


def solution(mesh):
    dims = (Z_COUNT, mesh.shape["lo"] // Z_COUNT, mesh.shape["hi"])
    in_specs = (
        P(None, ("hi", "lo")),
        P(("hi", "lo"), None),
        P(("hi", "lo"), None),
        P(None, ("hi", "lo"), None),
    )
    return jax.shard_map(
        functools.partial(per_device, dims), mesh=mesh, in_specs=in_specs,
        out_specs=P(None, ("hi", "lo")), check_vma=False
    )
```

```python
import functools

import jax
import jax.numpy as jnp
from jax import lax
from jax.experimental import pallas as pl
from jax.experimental.pallas import tpu as pltpu
from jax.sharding import PartitionSpec as P

ITERS = 3
Z_COUNT = 8
VMEM_BYTES = 60 * 1024 * 1024
MESH = pl.DeviceIdType.MESH
F32 = jnp.float32
BF16 = jnp.bfloat16
NN = (((1,), (0,)), ((), ()))
NT = (((1,), (1,)), ((), ()))


def bits(count):
    return count.bit_length() - 1


def spans(total, width):
    return [(low, min(width, total - low)) for low in range(0, total, width)]


def split(value):
    high = value.astype(BF16)
    low = (value - high.astype(F32)).astype(BF16)
    return high, low


def product(left, right, numbers):
    rows = left.shape[0] // 2
    both = lax.dot_general(left, right, numbers, preferred_element_type=F32)
    return both[:rows] + both[rows:]


def row_dot(a, b):
    return jnp.sum(a * b, axis=1, keepdims=True)


def pack_columns(columns):
    count = columns[0].shape[0]
    lane = lax.broadcasted_iota(jnp.int32, (count, 128), 1)
    row = lax.broadcasted_iota(jnp.int32, (count, 128), 0)
    spread = jnp.zeros((count, 128), F32)
    for kind, column in enumerate(columns):
        spread = jnp.where(lane == row + kind * count, column, spread)
    return jnp.sum(spread, axis=0, keepdims=True)


def unpack_column(packed, first, count):
    lane = lax.broadcasted_iota(jnp.int32, (count, 128), 1)
    row = lax.broadcasted_iota(jnp.int32, (count, 128), 0)
    picked = jnp.where(lane == row + first, packed, 0.0)
    return jnp.sum(picked, axis=1, keepdims=True)


def next_scalars(sums, rr_old, curvature):
    rr, rn, cross = sums
    if rr_old is None:
        beta = jnp.zeros_like(rr)
        curvature = rn
    else:
        beta = rr / rr_old
        curvature = rn + beta * cross + beta * beta * curvature
    return rr / curvature, beta, rr, curvature


def tree_steps(blocks, first_level, per_level):
    rows = blocks[0].shape[0]
    level_of_row = lax.broadcasted_iota(jnp.int32, (rows, 128), 0) // per_level
    products = jnp.zeros((rows, 128), F32)
    node_sums = []
    current = blocks
    level = first_level
    while len(current) > 1:
        node_sums.append(current)
        pairs = [(current[m], current[m + 1]) for m in range(0, len(current), 2)]
        total = sum(a * b for a, b in pairs)
        products = products + jnp.where(level_of_row == level, 2.0 * total, 0.0)
        current = [a + b for a, b in pairs]
        level += 1
    return node_sums, current[0], products


def fold_levels(products, per_level):
    column = jnp.sum(products, axis=1, keepdims=True)
    total = column[:per_level]
    for low in range(per_level, products.shape[0], per_level):
        total = total + column[low:low + per_level]
    return total


def kernel(dims, rhs_hbm, order_hbm, leaf_hbm, bases_hbm, out_ref, *scratch):
    nz, ny, nh = dims
    (rhs_ref, order_ref, blocks, basis, onehot, halves, sib_f32, sib_halves, residual, direction,
     image, far_dir, near, placed, pending, c_send, c_recv, l_send, l_recv, y_send, y_recv, h_send,
     h_recv, a_send, a_recv, b_send, b_recv, x_send, x_recv, s_send, sx_recv, sy_recv, sh_recv,
     sz_recv, l_now, l_image, c_now, c_image, far, sent, load_sem, send_sem, recv_sem) = scratch
    rhs_count, leaf = residual.shape
    levels = bases_hbm.shape[0]
    own = rhs_count // nz
    zb, yb, hb = bits(nz), bits(ny), bits(nh)
    c_rows = c_send.shape[2]
    h_low = yb * own // 8 * 8
    h_first = yb * own - h_low

    hi = lax.axis_index("hi")
    lo = lax.axis_index("lo")
    z = lax.rem(lo, nz)
    y = lo // nz

    z_steps = sorted(range(1, nz), key=lambda step: -min(step, nz - step))
    y_steps = sorted(range(1, ny), key=lambda step: -min(step, ny - step))
    h_steps = sorted(range(1, nh), key=lambda step: -min(step, nh - step))

    def z_device(step):
        return (hi, y * nz + lax.rem(z + step, nz))

    def y_device(step):
        return (hi, lax.rem(y + step, ny) * nz + z)

    def h_device(step):
        return (lax.rem(hi + step, nh), lo)

    upper = hi * ny + y
    masks = sorted(range(1, nh * ny), key=lambda mask: -mask.bit_count())

    def x_device(mask):
        other = upper
        for bit in range(bits(nh * ny)):
            if mask >> bit & 1:
                other = other + (1 - 2 * lax.rem(upper // (1 << bit), 2)) * (1 << bit)
        return (other // ny, lax.rem(other, ny) * nz + z)

    partners = [z_device(step) for step in z_steps]
    partners += [x_device(mask) for mask in masks]

    loads = []
    for level in range(levels):
        loads.append(pltpu.make_async_copy(
            bases_hbm.at[level], basis.at[:, pl.ds(128 * level, 128)], load_sem.at[level]))
    loads.append(pltpu.make_async_copy(leaf_hbm, blocks, load_sem.at[levels]))
    loads.insert(0, pltpu.make_async_copy(rhs_hbm, rhs_ref, load_sem.at[levels + 1]))
    loads.insert(0, pltpu.make_async_copy(order_hbm, order_ref, load_sem.at[levels + 2]))
    for load in loads:
        load.start()

    barrier = pltpu.get_barrier_semaphore()
    for partner in partners:
        pl.semaphore_signal(barrier, inc=1, device_id=partner, device_id_type=MESH)

    def send(src, dst, t, phase, partner):
        pltpu.make_async_remote_copy(
            src_ref=src, dst_ref=dst, send_sem=send_sem.at[t, phase],
            recv_sem=recv_sem.at[t, phase], device_id=partner, device_id_type=MESH,
        ).start()

    def await_recv(slots, t, phase):
        pltpu.make_async_copy(slots, slots, recv_sem.at[t, phase]).wait()

    def await_send(slots, t, phase):
        pltpu.make_async_copy(slots, slots, send_sem.at[t, phase]).wait()

    for load in loads[:2]:
        load.wait()
    order_row = order_ref[...]
    for low, width in spans(leaf, 128):
        place = lax.broadcasted_iota(jnp.int32, (width, leaf), 0) + low
        onehot[pl.ds(low, width), :] = jnp.where(place == order_row, 1.0, 0.0).astype(BF16)
    rhs_now = rhs_ref[...]
    for low, width in spans(leaf, 384):
        columns = pl.ds(low, width)
        tree = lax.dot_general(rhs_now, onehot[:, columns], NN, preferred_element_type=F32)
        residual[:, columns] = tree
        high, small = split(tree)
        halves[:, columns] = jnp.concatenate([high, small], axis=0)
    for load in loads[2:levels + 2]:
        load.wait()

    lane = lax.broadcasted_iota(jnp.int32, (own, 128), 1)
    row = lax.broadcasted_iota(jnp.int32, (own, 128), 0)
    mine = lane == row + rhs_count + z * own

    def add_dots(packed, products):
        spread = jnp.where(mine, fold_levels(products, own), 0.0)
        return packed + jnp.sum(spread, axis=0, keepdims=True)

    def send_projections(t, vector):
        projected = product(vector[...], basis[...], NN)
        for j in range(nz):
            for level in range(levels):
                target, at = (l_send, level) if level < zb else (c_send, level - zb)
                target[t, j, own * at:own * at + own, :] = (
                    projected[own * j:own * j + own, 128 * level:128 * level + 128])
        if t == 0:
            pl.semaphore_wait(barrier, len(partners))
        for step in z_steps:
            peer = lax.rem(z + step, nz)
            send(c_send.at[t, peer], c_recv.at[t, z], t, 0, z_device(step))
        for step in z_steps:
            peer = lax.rem(z + step, nz)
            send(l_send.at[t, peer], l_recv.at[t, z], t, 1, z_device(step))
        c_recv[t, z] = c_send[t, z]
        l_recv[t, z] = l_send[t, z]

    def near_and_dots(first):
        rr = jnp.zeros((rhs_count, 1), F32)
        rn = jnp.zeros((rhs_count, 1), F32)
        cross = jnp.zeros((rhs_count, 1), F32)
        for low, width in spans(leaf, 384):
            columns = pl.ds(low, width)
            near_now = product(halves[...], blocks[:, columns], NN)
            near[:, columns] = near_now
            r_now = residual[:, columns]
            rr = rr + row_dot(r_now, r_now)
            rn = rn + row_dot(r_now, near_now)
            if not first:
                cross = cross + row_dot(r_now, image[:, columns] + far_dir[:, columns])
                cross = cross + row_dot(direction[:, columns], near_now)
        return pack_columns([rr, rn, cross])

    def upper_sums(t, owned):
        await_recv(c_recv.at[t, pl.ds(0, nz - 1)], t, 0)
        total = c_recv[t, 0]
        for j in range(1, nz):
            total = total + c_recv[t, j]
        if t > 0:
            alpha, beta = (jnp.concatenate([v] * (c_rows // own), axis=0) for v in owned)
            if t > 1:
                total = total + beta * c_image[...]
            c_image[...] = total
            total = c_now[...] - alpha * total
        c_now[...] = total
        return total

    def lower_sums(t, owned):
        await_recv(l_recv.at[t, pl.ds(0, nz - 1)], t, 1)
        found = []
        for j in range(nz):
            block = l_recv[t, j]
            if t > 0:
                alpha, beta = (jnp.concatenate([v] * zb, axis=0) for v in owned)
                if t > 1:
                    block = block + beta * l_image[j]
                l_image[j] = block
                block = l_now[j] - alpha * block
            l_now[j] = block
            found.append(block)
        node_sums, _, products = tree_steps(found, 0, own)
        return node_sums, products

    def siblings(t, owned):
        if t == 0:
            loads[levels + 2].wait()
        packed = near_and_dots(t == 0)
        total = upper_sums(t, owned)
        for bit in range(yb + hb):
            x_send[t, bit] = total[own * bit:own * bit + own]
        for mask in masks:
            bit = mask.bit_length() - 1
            send(x_send.at[t, bit], x_recv.at[t, mask], t, 9, x_device(mask))
        node_sums, products = lower_sums(t, owned)
        packed = add_dots(packed, products)
        for j in range(nz):
            for level in range(zb):
                rows = slice(own * level, own * level + own)
                a_send[t, j, rows] = node_sums[level][(j >> level) ^ 1][rows]
        for step in z_steps:
            peer = lax.rem(z + step, nz)
            send(a_send.at[t, peer], a_recv.at[t, z], t, 4, z_device(step))
        a_recv[t, z] = a_send[t, z]

        await_recv(x_recv.at[t, pl.ds(1, nh * ny - 1)], t, 9)
        for bit in range(yb + hb):
            b_send[t, own * bit:own * bit + own] = sum(
                x_recv[t, mask] for mask in range(1 << bit, 2 << bit))
        for step in z_steps:
            send(b_send.at[t], b_recv.at[t, z], t, 7, z_device(step))
        b_recv[t, z] = b_send[t]
        packed = add_dots(packed, total * b_send[t])
        s_send[t, 0] = packed
        for mask in masks:
            send(s_send.at[t, 0], sx_recv.at[t, mask], t, 10, x_device(mask))
        if t > 0:
            for number in range(3):
                place_chunk(number)
        await_recv(sx_recv.at[t, pl.ds(1, nh * ny - 1)], t, 10)
        for mask in range(1, nh * ny):
            packed = packed + sx_recv[t, mask]
        s_send[t, 1] = packed
        for step in z_steps:
            send(s_send.at[t, 1], sz_recv.at[t, z], t, 8, z_device(step))
        sz_recv[t, z] = packed

        await_recv(a_recv.at[t, pl.ds(0, nz - 1)], t, 4)
        await_recv(b_recv.at[t, pl.ds(0, nz - 1)], t, 7)
        for j in range(nz):
            for level in range(levels):
                source, at = (a_recv, level) if level < zb else (b_recv, level - zb)
                sib_f32[own * j:own * j + own, 128 * level:128 * level + 128] = (
                    source[t, j, own * at:own * at + own, :])
        high, small = split(sib_f32[...])
        sib_halves[...] = jnp.concatenate([high, small], axis=0)
        for low, width in spans(leaf, 384):
            columns = pl.ds(low, width)
            far_now = product(sib_halves[...], basis[columns, :], NT)
            far[:, columns] = far_now
            high, small = split(near[:, columns] + far_now)
            sent[:, columns] = jnp.concatenate([high, small], axis=0)

    def finish(t, owned):
        packed = near_and_dots(False)
        total = upper_sums(t, owned)
        y_send[...] = total
        for step in y_steps:
            send(y_send, y_recv.at[y], t, 2, y_device(step))
        y_recv[y] = total
        _, products = lower_sums(t, owned)
        packed = add_dots(packed, products)
        s_send[t, 0] = packed
        for step in y_steps:
            send(s_send.at[t, 0], sy_recv.at[y], t, 3, y_device(step))
        sy_recv[y] = packed
        place_chunk(0)

        await_recv(y_recv.at[pl.ds(0, ny - 1)], t, 2)
        _, total, products = tree_steps([y_recv[j] for j in range(ny)], 0, own)
        h_send[...] = total[h_low:]
        for step in h_steps:
            send(h_send, h_recv.at[hi], t, 5, h_device(step))
        h_recv[hi] = total[h_low:]
        await_recv(sy_recv.at[pl.ds(0, ny - 1)], t, 3)
        packed = add_dots(sum(sy_recv[j] for j in range(ny)), products)
        s_send[t, 1] = packed
        for step in h_steps:
            send(s_send.at[t, 1], sh_recv.at[hi], t, 6, h_device(step))
        sh_recv[hi] = packed
        place_chunk(1)

        await_recv(h_recv.at[pl.ds(0, nh - 1)], t, 5)
        _, _, products = tree_steps([h_recv[j] for j in range(nh)], h_first // own, own)
        await_recv(sh_recv.at[pl.ds(0, nh - 1)], t, 6)
        packed = add_dots(sum(sh_recv[j] for j in range(nh)), products)
        s_send[t, 2] = packed
        for step in z_steps:
            send(s_send.at[t, 2], sz_recv.at[t, z], t, 8, z_device(step))
        sz_recv[t, z] = packed
        place_chunk(2)

    def total_scalars(t):
        await_recv(sz_recv.at[t, pl.ds(0, nz - 1)], t, 8)
        return sum(sz_recv[t, j] for j in range(nz))

    third = leaf // 3

    def place_chunk(number):
        for low, width in spans(third, 640):
            rows = pl.ds(number * third + low, width)
            pending[:, rows] = product(halves[...], onehot[rows, :], NT)

    state, owned_state, owned = (None, None), (None, None), None
    send_projections(0, halves)
    for t in range(ITERS):
        if t < ITERS - 1:
            siblings(t, owned)
            send_projections(t + 1, sent)
        else:
            finish(t, owned)
        packed = total_scalars(t)
        sums = [unpack_column(packed, kind * rhs_count, rhs_count) for kind in range(3)]
        alpha, beta, *state = next_scalars(sums, *state)
        here = rhs_now.astype(F32) if t == 0 else pending[...] + beta * placed[...]
        if t == ITERS - 1:
            out_ref[...] = out_ref[...] + alpha * here
            break
        sums = [unpack_column(packed, kind * rhs_count + z * own, own) for kind in range(3)]
        *owned, rr_owned, curvature = next_scalars(sums, *owned_state)
        owned_state = rr_owned, curvature
        for low, width in spans(leaf, 384):
            columns = pl.ds(low, width)
            r_now = residual[:, columns]
            far_now = far[:, columns]
            image_now = near[:, columns] + far_now
            direction_now = r_now
            if t > 0:
                far_now = far_now + beta * far_dir[:, columns]
                image_now = image_now + beta * image[:, columns]
                direction_now = direction_now + beta * direction[:, columns]
            far_dir[:, columns] = far_now
            image[:, columns] = image_now
            direction[:, columns] = direction_now
            r_next = r_now - alpha * image_now
            residual[:, columns] = r_next
            high, small = split(r_next)
            halves[:, columns] = jnp.concatenate([high, small], axis=0)
        placed[...] = here
        out_ref[...] = alpha * here if t == 0 else out_ref[...] + alpha * here

    for t in range(ITERS):
        await_send(c_recv.at[t, pl.ds(0, nz - 1)], t, 0)
        await_send(l_recv.at[t, pl.ds(0, nz - 1)], t, 1)
        await_send(sz_recv.at[t, pl.ds(0, nz - 1)], t, 8)
        if t < ITERS - 1:
            await_send(x_recv.at[t, pl.ds(1, nh * ny - 1)], t, 9)
            await_send(sx_recv.at[t, pl.ds(1, nh * ny - 1)], t, 10)
            await_send(a_recv.at[t, pl.ds(0, nz - 1)], t, 4)
            await_send(b_recv.at[t, pl.ds(0, nz - 1)], t, 7)
        else:
            await_send(y_recv.at[pl.ds(0, ny - 1)], t, 2)
            await_send(sy_recv.at[pl.ds(0, ny - 1)], t, 3)
            await_send(h_recv.at[pl.ds(0, nh - 1)], t, 5)
            await_send(sh_recv.at[pl.ds(0, nh - 1)], t, 6)


def per_device(dims, right_side, point_order, leaf_blocks, bases):
    nz, ny, nh = dims
    rhs_count, leaf = right_side.shape
    levels = bases.shape[0]
    own = rhs_count // nz
    yb = bits(ny)
    l_rows = bits(nz) * own
    c_rows = levels * own - l_rows
    h_rows = c_rows - yb * own // 8 * 8
    vector = pltpu.VMEM((rhs_count, leaf), F32)

    def buffer(*shape):
        return pltpu.VMEM((ITERS, *shape, 128), F32)

    def once(*shape):
        return pltpu.VMEM((*shape, 128), F32)

    scratch = [
        pltpu.VMEM((rhs_count, leaf), BF16),
        pltpu.VMEM((1, leaf), jnp.int32),
        pltpu.VMEM((leaf, leaf), BF16),
        pltpu.VMEM((leaf, 128 * levels), BF16),
        pltpu.VMEM((leaf, leaf), BF16),
        pltpu.VMEM((2 * rhs_count, leaf), BF16),
        pltpu.VMEM((rhs_count, 128 * levels), F32),
        pltpu.VMEM((2 * rhs_count, 128 * levels), BF16),
        vector, vector, vector, vector, vector, vector, vector,
        buffer(nz, c_rows), buffer(nz, c_rows),
        buffer(nz, l_rows), buffer(nz, l_rows),
        once(c_rows), once(ny, c_rows),
        once(h_rows), once(nh, h_rows),
        buffer(nz, l_rows), buffer(nz, l_rows),
        buffer(c_rows), buffer(nz, c_rows),
        buffer(levels - bits(nz), own), buffer(nh * ny, own),
        buffer(3, 1), buffer(nh * ny, 1), once(ny, 1), once(nh, 1), buffer(nz, 1),
        once(nz, l_rows), once(nz, l_rows), once(c_rows), once(c_rows),
        vector, pltpu.VMEM((2 * rhs_count, leaf), BF16),
        pltpu.SemaphoreType.DMA((levels + 3,)),
        pltpu.SemaphoreType.DMA((ITERS, 11)),
        pltpu.SemaphoreType.DMA((ITERS, 11)),
    ]
    return pl.pallas_call(
        functools.partial(kernel, dims),
        out_shape=jax.ShapeDtypeStruct((rhs_count, leaf), F32),
        in_specs=[
            pl.BlockSpec(memory_space=pl.ANY),
            pl.BlockSpec(memory_space=pl.ANY),
            pl.BlockSpec(memory_space=pl.ANY),
            pl.BlockSpec(memory_space=pl.ANY),
        ],
        out_specs=pl.BlockSpec(memory_space=pltpu.VMEM),
        scratch_shapes=scratch,
        compiler_params=pltpu.CompilerParams(
            collective_id=0, has_side_effects=True, vmem_limit_bytes=VMEM_BYTES
        ),
        name="tree_cg",
    )(right_side, point_order, leaf_blocks, bases)


def solution(mesh):
    dims = (Z_COUNT, mesh.shape["lo"] // Z_COUNT, mesh.shape["hi"])
    in_specs = (
        P(None, ("hi", "lo")),
        P(("hi", "lo"), None),
        P(("hi", "lo"), None),
        P(None, ("hi", "lo"), None),
    )
    return jax.shard_map(
        functools.partial(per_device, dims), mesh=mesh, in_specs=in_specs,
        out_specs=P(None, ("hi", "lo")), check_vma=False
    )
```

```python
import functools

import jax
import jax.numpy as jnp
from jax import lax
from jax.experimental import pallas as pl
from jax.experimental.pallas import tpu as pltpu
from jax.sharding import PartitionSpec as P

ITERS = 3
Z_COUNT = 8
VMEM_BYTES = 60 * 1024 * 1024
MESH = pl.DeviceIdType.MESH
F32 = jnp.float32
BF16 = jnp.bfloat16
NN = (((1,), (0,)), ((), ()))
NT = (((1,), (1,)), ((), ()))


def bits(count):
    return count.bit_length() - 1


def spans(total, width):
    return [(low, min(width, total - low)) for low in range(0, total, width)]


def split(value):
    high = value.astype(BF16)
    low = (value - high.astype(F32)).astype(BF16)
    return high, low


def product(left, right, numbers):
    rows = left.shape[0] // 2
    both = lax.dot_general(left, right, numbers, preferred_element_type=F32)
    return both[:rows] + both[rows:]


def row_dot(a, b):
    return jnp.sum(a * b, axis=1, keepdims=True)


def pack_columns(columns):
    count = columns[0].shape[0]
    lane = lax.broadcasted_iota(jnp.int32, (count, 128), 1)
    row = lax.broadcasted_iota(jnp.int32, (count, 128), 0)
    spread = jnp.zeros((count, 128), F32)
    for kind, column in enumerate(columns):
        spread = jnp.where(lane == row + kind * count, column, spread)
    return jnp.sum(spread, axis=0, keepdims=True)


def unpack_column(packed, first, count):
    lane = lax.broadcasted_iota(jnp.int32, (count, 128), 1)
    row = lax.broadcasted_iota(jnp.int32, (count, 128), 0)
    picked = jnp.where(lane == row + first, packed, 0.0)
    return jnp.sum(picked, axis=1, keepdims=True)


def next_scalars(sums, rr_old, curvature):
    rr, rn, cross = sums
    if rr_old is None:
        beta = jnp.zeros_like(rr)
        curvature = rn
    else:
        beta = rr / rr_old
        curvature = rn + beta * cross + beta * beta * curvature
    return rr / curvature, beta, rr, curvature


def tree_steps(blocks, first_level, per_level):
    rows = blocks[0].shape[0]
    level_of_row = lax.broadcasted_iota(jnp.int32, (rows, 128), 0) // per_level
    products = jnp.zeros((rows, 128), F32)
    node_sums = []
    current = blocks
    level = first_level
    while len(current) > 1:
        node_sums.append(current)
        pairs = [(current[m], current[m + 1]) for m in range(0, len(current), 2)]
        total = sum(a * b for a, b in pairs)
        products = products + jnp.where(level_of_row == level, 2.0 * total, 0.0)
        current = [a + b for a, b in pairs]
        level += 1
    return node_sums, current[0], products


def fold_levels(products, per_level):
    column = jnp.sum(products, axis=1, keepdims=True)
    total = column[:per_level]
    for low in range(per_level, products.shape[0], per_level):
        total = total + column[low:low + per_level]
    return total


def kernel(dims, rhs_hbm, order_hbm, leaf_hbm, bases_hbm, out_ref, *scratch):
    nz, ny, nh = dims
    (rhs_ref, order_ref, blocks, basis, basis_t, onehot, halves, sib_f32, sib_halves, residual, direction,
     image, far_dir, near, placed, pending, c_send, c_recv, l_send, l_recv, y_send, y_recv, h_send,
     h_recv, a_send, a_recv, b_send, b_recv, x_send, x_recv, s_send, sx_recv, sy_recv, sh_recv,
     sz_recv, l_now, l_image, c_now, c_image, far, sent, load_sem, send_sem, recv_sem) = scratch
    rhs_count, leaf = residual.shape
    levels = bases_hbm.shape[0]
    own = rhs_count // nz
    zb, yb, hb = bits(nz), bits(ny), bits(nh)
    c_rows = c_send.shape[2]
    h_low = yb * own // 8 * 8
    h_first = yb * own - h_low

    hi = lax.axis_index("hi")
    lo = lax.axis_index("lo")
    z = lax.rem(lo, nz)
    y = lo // nz

    z_steps = sorted(range(1, nz), key=lambda step: -min(step, nz - step))
    y_steps = sorted(range(1, ny), key=lambda step: -min(step, ny - step))
    h_steps = sorted(range(1, nh), key=lambda step: -min(step, nh - step))

    def z_device(step):
        return (hi, y * nz + lax.rem(z + step, nz))

    def y_device(step):
        return (hi, lax.rem(y + step, ny) * nz + z)

    def h_device(step):
        return (lax.rem(hi + step, nh), lo)

    upper = hi * ny + y
    masks = sorted(range(1, nh * ny), key=lambda mask: -(
        2 * (0, 1, 2, 1)[mask % ny] + 2 * (0, 1, 2, 1)[mask // ny // 2] + mask // ny % 2))

    def x_device(mask):
        other = upper
        for bit in range(bits(nh * ny)):
            if mask >> bit & 1:
                other = other + (1 - 2 * lax.rem(upper // (1 << bit), 2)) * (1 << bit)
        return (other // ny, lax.rem(other, ny) * nz + z)

    partners = [z_device(step) for step in z_steps]
    partners += [x_device(mask) for mask in masks]

    barrier = pltpu.get_barrier_semaphore()
    for partner in partners:
        pl.semaphore_signal(barrier, inc=1, device_id=partner, device_id_type=MESH)

    loads = []
    for level in range(levels):
        loads.append(pltpu.make_async_copy(
            bases_hbm.at[level], basis.at[:, pl.ds(128 * level, 128)], load_sem.at[level]))
    loads.append(pltpu.make_async_copy(leaf_hbm, blocks, load_sem.at[levels]))
    loads.insert(0, pltpu.make_async_copy(rhs_hbm, rhs_ref, load_sem.at[levels + 1]))
    loads.insert(0, pltpu.make_async_copy(order_hbm, order_ref, load_sem.at[levels + 2]))
    for load in loads:
        load.start()

    def send(src, dst, t, phase, partner):
        pltpu.make_async_remote_copy(
            src_ref=src, dst_ref=dst, send_sem=send_sem.at[t, phase],
            recv_sem=recv_sem.at[t, phase], device_id=partner, device_id_type=MESH,
        ).start()

    def await_recv(slots, t, phase):
        pltpu.make_async_copy(slots, slots, recv_sem.at[t, phase]).wait()

    def await_send(slots, t, phase):
        pltpu.make_async_copy(slots, slots, send_sem.at[t, phase]).wait()

    for load in loads[:2]:
        load.wait()
    order_row = order_ref[...]
    for low, width in spans(leaf, 128):
        place = lax.broadcasted_iota(jnp.int32, (width, leaf), 0) + low
        onehot[pl.ds(low, width), :] = jnp.where(place == order_row, 1.0, 0.0).astype(BF16)
    rhs_now = rhs_ref[...]
    for low, width in spans(leaf, 384):
        columns = pl.ds(low, width)
        tree = lax.dot_general(rhs_now, onehot[:, columns], NN, preferred_element_type=F32)
        residual[:, columns] = tree
        high, small = split(tree)
        halves[:, columns] = jnp.concatenate([high, small], axis=0)
    for load in loads[2:levels + 2]:
        load.wait()

    lane = lax.broadcasted_iota(jnp.int32, (own, 128), 1)
    row = lax.broadcasted_iota(jnp.int32, (own, 128), 0)
    mine = lane == row + rhs_count + z * own

    def add_dots(packed, products):
        spread = jnp.where(mine, fold_levels(products, own), 0.0)
        return packed + jnp.sum(spread, axis=0, keepdims=True)

    def send_projections(t, vector):
        parts = ((c_send, c_recv, zb, levels), (l_send, l_recv, 0, zb))
        for phase, (source, target, low, stop) in enumerate(parts):
            projected = product(vector[...], basis[:, 128 * low:128 * stop], NN)
            for j in range(nz):
                for at in range(stop - low):
                    source[t, j, own * at:own * at + own, :] = (
                        projected[own * j:own * j + own, 128 * at:128 * at + 128])
            if t == 0 and phase == 0:
                pl.semaphore_wait(barrier, len(partners))
            for step in z_steps:
                peer = lax.rem(z + step, nz)
                send(source.at[t, peer], target.at[t, z], t, phase, z_device(step))
        c_recv[t, z] = c_send[t, z]
        l_recv[t, z] = l_send[t, z]

    def near_and_dots(first):
        rr = jnp.zeros((rhs_count, 1), F32)
        rn = jnp.zeros((rhs_count, 1), F32)
        cross = jnp.zeros((rhs_count, 1), F32)
        for low, width in spans(leaf, 512):
            columns = pl.ds(low, width)
            near_now = product(halves[...], blocks[:, columns], NN)
            near[:, columns] = near_now
            r_now = residual[:, columns]
            rr = rr + row_dot(r_now, r_now)
            rn = rn + row_dot(r_now, near_now)
            if not first:
                cross = cross + row_dot(r_now, image[:, columns] + far_dir[:, columns])
                cross = cross + row_dot(direction[:, columns], near_now)
        return pack_columns([rr, rn, cross])

    def upper_sums(t, owned):
        await_recv(c_recv.at[t, pl.ds(0, nz - 1)], t, 0)
        total = c_recv[t, 0]
        for j in range(1, nz):
            total = total + c_recv[t, j]
        if t > 0:
            alpha, beta = (jnp.concatenate([v] * (c_rows // own), axis=0) for v in owned)
            if t > 1:
                total = total + beta * c_image[...]
            c_image[...] = total
            total = c_now[...] - alpha * total
        c_now[...] = total
        return total

    def lower_sums(t, owned):
        await_recv(l_recv.at[t, pl.ds(0, nz - 1)], t, 1)
        found = []
        for j in range(nz):
            block = l_recv[t, j]
            if t > 0:
                alpha, beta = (jnp.concatenate([v] * zb, axis=0) for v in owned)
                if t > 1:
                    block = block + beta * l_image[j]
                l_image[j] = block
                block = l_now[j] - alpha * block
            l_now[j] = block
            found.append(block)
        node_sums, _, products = tree_steps(found, 0, own)
        return node_sums, products

    def transpose_bases(first, stop):
        for level in range(first, stop):
            for low, width in spans(leaf, 128):
                part = basis[pl.ds(low, width), 128 * level:128 * level + 128].astype(F32)
                basis_t[128 * level:128 * level + 128, pl.ds(low, width)] = part.T.astype(BF16)

    def gather_siblings(source, t, first, stop):
        for j in range(nz):
            for level in range(first, stop):
                at = own * (level - first)
                sib_f32[own * j:own * j + own, 128 * level:128 * level + 128] = (
                    source[t, j, at:at + own, :])
        columns = slice(128 * first, 128 * stop)
        high, small = split(sib_f32[:, columns])
        sib_halves[:, columns] = jnp.concatenate([high, small], axis=0)

    def siblings(t, owned):
        if t == 0:
            loads[levels + 2].wait()
        packed = near_and_dots(True) if t == 0 else None
        total = upper_sums(t, owned)
        for bit in range(yb + hb):
            x_send[t, bit] = total[own * bit:own * bit + own]
        for mask in masks:
            bit = mask.bit_length() - 1
            send(x_send.at[t, bit], x_recv.at[t, mask], t, 9, x_device(mask))
        node_sums, products = lower_sums(t, owned)
        for j in range(nz):
            for level in range(zb):
                rows = slice(own * level, own * level + own)
                a_send[t, j, rows] = node_sums[level][(j >> level) ^ 1][rows]
        for step in z_steps:
            peer = lax.rem(z + step, nz)
            send(a_send.at[t, peer], a_recv.at[t, z], t, 4, z_device(step))
        a_recv[t, z] = a_send[t, z]
        if t == 0:
            transpose_bases(0, levels // 2)
        else:
            packed = near_and_dots(False)
        packed = add_dots(packed, products)
        await_recv(x_recv.at[t, pl.ds(1, nh * ny - 1)], t, 9)
        for bit in range(yb + hb):
            b_send[t, own * bit:own * bit + own] = sum(
                x_recv[t, mask] for mask in range(1 << bit, 2 << bit))
        for step in z_steps:
            send(b_send.at[t], b_recv.at[t, z], t, 7, z_device(step))
        b_recv[t, z] = b_send[t]
        packed = add_dots(packed, total * b_send[t])
        s_send[t, 0] = packed
        for mask in masks:
            send(s_send.at[t, 0], sx_recv.at[t, mask], t, 10, x_device(mask))
        if t == 0:
            transpose_bases(levels // 2, levels)
        await_recv(a_recv.at[t, pl.ds(0, nz - 1)], t, 4)
        gather_siblings(a_recv, t, 0, zb)
        for low, width in spans(leaf, 512):
            columns = pl.ds(low, width)
            far[:, columns] = product(sib_halves[:, :128 * zb], basis_t[:128 * zb, columns], NN)
        if t > 0:
            for number in range(3):
                place_chunk(number)
        await_recv(sx_recv.at[t, pl.ds(1, nh * ny - 1)], t, 10)
        for mask in range(1, nh * ny):
            packed = packed + sx_recv[t, mask]
        s_send[t, 1] = packed
        for step in z_steps:
            send(s_send.at[t, 1], sz_recv.at[t, z], t, 8, z_device(step))
        sz_recv[t, z] = packed

        await_recv(b_recv.at[t, pl.ds(0, nz - 1)], t, 7)
        gather_siblings(b_recv, t, zb, levels)
        for low, width in spans(leaf, 512):
            columns = pl.ds(low, width)
            upper_part = product(sib_halves[:, 128 * zb:], basis_t[128 * zb:, columns], NN)
            far_now = far[:, columns] + upper_part
            far[:, columns] = far_now
            high, small = split(near[:, columns] + far_now)
            sent[:, columns] = jnp.concatenate([high, small], axis=0)

    def finish(t, owned):
        packed = near_and_dots(False)
        total = upper_sums(t, owned)
        y_send[...] = total
        for step in y_steps:
            send(y_send, y_recv.at[y], t, 2, y_device(step))
        y_recv[y] = total
        _, products = lower_sums(t, owned)
        packed = add_dots(packed, products)
        s_send[t, 0] = packed
        for step in y_steps:
            send(s_send.at[t, 0], sy_recv.at[y], t, 3, y_device(step))
        sy_recv[y] = packed
        place_chunk(0)

        await_recv(y_recv.at[pl.ds(0, ny - 1)], t, 2)
        _, total, products = tree_steps([y_recv[j] for j in range(ny)], 0, own)
        h_send[...] = total[h_low:]
        for step in h_steps:
            send(h_send, h_recv.at[hi], t, 5, h_device(step))
        h_recv[hi] = total[h_low:]
        await_recv(sy_recv.at[pl.ds(0, ny - 1)], t, 3)
        packed = add_dots(sum(sy_recv[j] for j in range(ny)), products)
        s_send[t, 1] = packed
        for step in h_steps:
            send(s_send.at[t, 1], sh_recv.at[hi], t, 6, h_device(step))
        sh_recv[hi] = packed
        place_chunk(1)

        await_recv(h_recv.at[pl.ds(0, nh - 1)], t, 5)
        _, _, products = tree_steps([h_recv[j] for j in range(nh)], h_first // own, own)
        await_recv(sh_recv.at[pl.ds(0, nh - 1)], t, 6)
        packed = add_dots(sum(sh_recv[j] for j in range(nh)), products)
        s_send[t, 2] = packed
        for step in z_steps:
            send(s_send.at[t, 2], sz_recv.at[t, z], t, 8, z_device(step))
        sz_recv[t, z] = packed
        place_chunk(2)

    def total_scalars(t):
        await_recv(sz_recv.at[t, pl.ds(0, nz - 1)], t, 8)
        return sum(sz_recv[t, j] for j in range(nz))

    third = leaf // 3

    def place_chunk(number):
        for low, width in spans(third, 640):
            rows = pl.ds(number * third + low, width)
            pending[:, rows] = product(halves[...], onehot[rows, :], NT)

    state, owned_state, owned = (None, None), (None, None), None
    send_projections(0, halves)
    for t in range(ITERS):
        if t < ITERS - 1:
            siblings(t, owned)
            send_projections(t + 1, sent)
        else:
            finish(t, owned)
        packed = total_scalars(t)
        sums = [unpack_column(packed, kind * rhs_count, rhs_count) for kind in range(3)]
        alpha, beta, *state = next_scalars(sums, *state)
        here = rhs_now.astype(F32) if t == 0 else pending[...] + beta * placed[...]
        if t == ITERS - 1:
            out_ref[...] = out_ref[...] + alpha * here
            break
        sums = [unpack_column(packed, kind * rhs_count + z * own, own) for kind in range(3)]
        *owned, rr_owned, curvature = next_scalars(sums, *owned_state)
        owned_state = rr_owned, curvature
        for low, width in spans(leaf, 384):
            columns = pl.ds(low, width)
            r_now = residual[:, columns]
            far_now = far[:, columns]
            image_now = near[:, columns] + far_now
            direction_now = r_now
            if t > 0:
                far_now = far_now + beta * far_dir[:, columns]
                image_now = image_now + beta * image[:, columns]
                direction_now = direction_now + beta * direction[:, columns]
            far_dir[:, columns] = far_now
            image[:, columns] = image_now
            direction[:, columns] = direction_now
            r_next = r_now - alpha * image_now
            residual[:, columns] = r_next
            high, small = split(r_next)
            halves[:, columns] = jnp.concatenate([high, small], axis=0)
        placed[...] = here
        out_ref[...] = alpha * here if t == 0 else out_ref[...] + alpha * here

    for t in range(ITERS):
        await_send(c_recv.at[t, pl.ds(0, nz - 1)], t, 0)
        await_send(l_recv.at[t, pl.ds(0, nz - 1)], t, 1)
        await_send(sz_recv.at[t, pl.ds(0, nz - 1)], t, 8)
        if t < ITERS - 1:
            await_send(x_recv.at[t, pl.ds(1, nh * ny - 1)], t, 9)
            await_send(sx_recv.at[t, pl.ds(1, nh * ny - 1)], t, 10)
            await_send(a_recv.at[t, pl.ds(0, nz - 1)], t, 4)
            await_send(b_recv.at[t, pl.ds(0, nz - 1)], t, 7)
        else:
            await_send(y_recv.at[pl.ds(0, ny - 1)], t, 2)
            await_send(sy_recv.at[pl.ds(0, ny - 1)], t, 3)
            await_send(h_recv.at[pl.ds(0, nh - 1)], t, 5)
            await_send(sh_recv.at[pl.ds(0, nh - 1)], t, 6)


def per_device(dims, right_side, point_order, leaf_blocks, bases):
    nz, ny, nh = dims
    rhs_count, leaf = right_side.shape
    levels = bases.shape[0]
    own = rhs_count // nz
    yb = bits(ny)
    l_rows = bits(nz) * own
    c_rows = levels * own - l_rows
    h_rows = c_rows - yb * own // 8 * 8
    vector = pltpu.VMEM((rhs_count, leaf), F32)

    def buffer(*shape):
        return pltpu.VMEM((ITERS, *shape, 128), F32)

    def once(*shape):
        return pltpu.VMEM((*shape, 128), F32)

    scratch = [
        pltpu.VMEM((rhs_count, leaf), BF16),
        pltpu.VMEM((1, leaf), jnp.int32),
        pltpu.VMEM((leaf, leaf), BF16),
        pltpu.VMEM((leaf, 128 * levels), BF16),
        pltpu.VMEM((128 * levels, leaf), BF16),
        pltpu.VMEM((leaf, leaf), BF16),
        pltpu.VMEM((2 * rhs_count, leaf), BF16),
        pltpu.VMEM((rhs_count, 128 * levels), F32),
        pltpu.VMEM((2 * rhs_count, 128 * levels), BF16),
        vector, vector, vector, vector, vector, vector, vector,
        buffer(nz, c_rows), buffer(nz, c_rows),
        buffer(nz, l_rows), buffer(nz, l_rows),
        once(c_rows), once(ny, c_rows),
        once(h_rows), once(nh, h_rows),
        buffer(nz, l_rows), buffer(nz, l_rows),
        buffer(c_rows), buffer(nz, c_rows),
        buffer(levels - bits(nz), own), buffer(nh * ny, own),
        buffer(3, 1), buffer(nh * ny, 1), once(ny, 1), once(nh, 1), buffer(nz, 1),
        once(nz, l_rows), once(nz, l_rows), once(c_rows), once(c_rows),
        vector, pltpu.VMEM((2 * rhs_count, leaf), BF16),
        pltpu.SemaphoreType.DMA((levels + 3,)),
        pltpu.SemaphoreType.DMA((ITERS, 11)),
        pltpu.SemaphoreType.DMA((ITERS, 11)),
    ]
    return pl.pallas_call(
        functools.partial(kernel, dims),
        out_shape=jax.ShapeDtypeStruct((rhs_count, leaf), F32),
        in_specs=[
            pl.BlockSpec(memory_space=pl.ANY),
            pl.BlockSpec(memory_space=pl.ANY),
            pl.BlockSpec(memory_space=pl.ANY),
            pl.BlockSpec(memory_space=pl.ANY),
        ],
        out_specs=pl.BlockSpec(memory_space=pltpu.VMEM),
        scratch_shapes=scratch,
        compiler_params=pltpu.CompilerParams(
            collective_id=0, has_side_effects=True, vmem_limit_bytes=VMEM_BYTES
        ),
        name="tree_cg",
    )(right_side, point_order, leaf_blocks, bases)


def solution(mesh):
    dims = (Z_COUNT, mesh.shape["lo"] // Z_COUNT, mesh.shape["hi"])
    in_specs = (
        P(None, ("hi", "lo")),
        P(("hi", "lo"), None),
        P(("hi", "lo"), None),
        P(None, ("hi", "lo"), None),
    )
    return jax.shard_map(
        functools.partial(per_device, dims), mesh=mesh, in_specs=in_specs,
        out_specs=P(None, ("hi", "lo")), check_vma=False
    )
```
